128 devices in a mesh: dev: 128 (over x, y, z, core).
Axes of the slice: x: 4, y: 4, z: 4, core: 2. Of those that a mesh axis runs over, the one named last changes fastest.
Arguments:
- positions: float32 [3, 524288], P(None, 'dev'), may hold values from 0 to 1
- velocities: float32 [3, 524288], P(None, 'dev'), may hold values from -3 to 3
- masses: float32 [524288], P('dev'), may hold values from 0.25 to 4
- samples: float32 [3, 4194304], P(None, 'dev'), may hold values from 0 to 1
- sample_mass: float32 [4194304], P('dev'), may hold values from 0.5 to 2
- start_potential: float32 [4194304], P('dev'), may hold values from -0.1 to 2.9
- route_owner: int32 [4096, 4], P('dev'), may hold values from 0 to 127, all different within a row; in each aligned block of 32 rows (0 to 31, 32 to 63, ...) at most 2 rows name the same one
- route_tile: int32 [4096, 4], P('dev'), may hold values from 0 to 63
- live_count: int32 [4096], P('dev'), may hold values from 3 to 4
Outputs:
- new_position: float32 [3, 524288], P(None, 'dev')
- new_velocity: float32 [3, 524288], P(None, 'dev')
The draws below stay inside these ranges and needn't reach their ends.
Inputs may be any that keep to these rules, and one draw needn't show every extreme that they name: `route_owner`: each row names 4 different devices; among the 32 rows of one device no device is named more than 2 times, and some device is named exactly 2 times.
All inputs are finite; a program needn't handle non-finite values.
Results may differ from the reference program's by a relative error of at most 0.0003.
Values sent between devices are 32-bit elements; how exact they have to be, the bound alone decides.
A program may use at most 64 MiB of HBM per device.

```python
import math
import jax
import jax.numpy as jnp
import numpy as np
from jax import lax

BLK = 128
TILE = 512
K = 4
ITERS = 2
PB_DEV = 32
NT_DEV = 64
BLOCKS = 4096
TILES = 8192
PARTICLES = 524288
SAMPLES = 4194304
CAP = 2
N_DEV = 128


def draw_samples(key, part):
    base = jax.random.uniform(jax.random.fold_in(key, 23), (3, TILES, TILE), jnp.float32, 0.0, 1.0)
    return base.reshape(3, SAMPLES)


def draw_start_potential(key, part):
    noise_key = jax.random.fold_in(jax.random.fold_in(key, 17), 0)
    base = 0.02 * jax.random.truncated_normal(noise_key, -4.0, 4.0, (TILES, TILE), jnp.float32)
    return base.reshape(SAMPLES)


def with_ends(result, own_key, smallest, high):
    index_at = [jax.random.randint(jax.random.fold_in(own_key, axis), (), 0, length) for axis, length in enumerate(result.shape)]
    widest = result.shape.index(max(result.shape))
    next_to = index_at[:widest] + [(index_at[widest] + 1) % result.shape[widest]] + index_at[widest + 1:]
    return result.at[tuple(index_at)].set(smallest).at[tuple(next_to)].set(high)


def block_scale(rng, extent, shards, least, largest):
    level = 1.0
    for position, shards_of in shards:
        draws = jax.random.uniform(jax.random.fold_in(jax.random.fold_in(rng, 6), position), (shards_of,), jnp.float32, least / len(shards), largest / len(shards))
        level = level * jnp.repeat(jnp.exp(draws), extent[position] // shards_of).reshape((-1,) + (1,) * (len(extent) - 1 - position))
    return level


def shared_out(own_key, own, number, rows, amount, top, most, lean):
    sequence = jax.random.permutation(own_key, amount)
    heavy_load, common = portions_of(amount, rows * top, most, lean, True), portions_of(amount, rows * top, most, lean, False)
    places = jnp.arange(amount)

    def named(tallies, rotation):
        used = int((tallies > 0).sum())
        fixed = max(1, used // 4)
        passed = fixed + (places - fixed + rotation * (used - fixed)) % max(1, amount - fixed)
        return jnp.zeros((amount,), jnp.int32).at[sequence[jnp.where(places < fixed, places, passed)]].set(jnp.asarray(tallies, jnp.int32))

    tallies = jnp.where(number % 4 == 0, named(heavy_load, number // 4), named(common, number - number // 4 - 1))
    mixed = jax.random.permutation(jax.random.fold_in(own, 3), amount)
    donor, sink = mixed[0:amount // 2 * 2:2], mixed[1:amount // 2 * 2:2]
    margin = jnp.minimum(tallies[donor] - 1, most - tallies[sink]) // 2
    margin = jnp.where((donor == sequence[0]) | (sink == sequence[0]) | (tallies[sink] == 0), 0, jnp.maximum(margin, 0))
    passed = jax.random.randint(jax.random.fold_in(own, 4), (amount // 2,), 0, 1 << 20) % (margin + 1)
    tallies = tallies.at[donor].add(-passed).at[sink].add(passed)
    labels = jnp.searchsorted(jnp.cumsum(tallies), jnp.arange(rows * top), side="right").astype(jnp.int32)
    table = labels.reshape(top, rows).T
    table = table[jax.random.permutation(jax.random.fold_in(own, 1), rows)]
    rotation = jax.random.randint(jax.random.fold_in(own, 2), (rows, 1), 0, top)
    return jnp.take_along_axis(table, (jnp.arange(top)[None, :] + rotation) % top, axis=1)


def portions_of(count, total, bound, lean, full):
    loads = [(1 << 20) // math.isqrt(rank ** lean) + 1 for rank in range(1, count + 1)]
    largest = bound if full else min(bound, max(-(-total // count), total * loads[0] // sum(loads)))
    least = 1 if total - largest >= count - 1 else 0
    holding, surplus = [largest] + [least] * (count - 1), total - largest - least * (count - 1)
    while surplus > 0:
        movable = [i for i in range(1, count) if holding[i] < largest] or [i for i in range(1, count) if holding[i] < bound]
        mass, budget = sum([loads[i] for i in movable]), surplus
        for i in movable:
            addition = min(bound - holding[i], max(1, budget * loads[i] // mass), surplus)
            holding[i] = holding[i] + addition
            surplus = surplus - addition
    return np.array(holding)


def bell_draw(key, dims, scale, most, cuts=(), kind=jnp.bfloat16):
    values = jax.random.normal(key, dims, jnp.float32) * scale
    if len(cuts) > 0:
        values = block_scale(key, dims, cuts, -0.22, 0.18) * values
    return jnp.clip(values, min=-most, max=most).astype(kind)


def setup_inputs(seed: int = 0) -> dict:
    key_of = jax.random.split(jax.random.key(seed), 10)
    positions = jnp.clip(1.0 * jax.random.uniform(key_of[0], (3, PARTICLES), jnp.float32) ** block_scale(key_of[0], (3, PARTICLES), ((1, 128),), -0.2, 0.2), 0.0, 1.0)
    velocities = bell_draw(key_of[1], (3, PARTICLES), 0.5, 3.0, ((1, 128),), jnp.float32)
    masses = jnp.clip(jnp.exp(math.log(4.0) - 2.7725887 * jax.random.uniform(key_of[2], (PARTICLES,), jnp.float32) ** block_scale(key_of[2], (PARTICLES,), ((0, 128),), -0.2, 0.2)), 0.25, 4.0)
    samples = draw_samples(jax.random.fold_in(key_of[9], 71), 0)
    sample_mass = jnp.clip(jnp.exp(math.log(2.0) - 1.3862944 * jax.random.uniform(key_of[4], (SAMPLES,), jnp.float32) ** block_scale(key_of[4], (SAMPLES,), ((0, 128),), -0.2, 0.2)), 0.5, 2.0)
    start_potential = draw_start_potential(jax.random.fold_in(key_of[9], 71), 0)
    route_owner_keys = jax.random.split(jax.random.fold_in(key_of[6], 1), BLOCKS // PB_DEV)
    route_owner_turns = jax.random.permutation(jax.random.fold_in(key_of[6], 3), BLOCKS // PB_DEV)
    route_owner = jax.vmap(lambda own, number: shared_out(jax.random.fold_in(key_of[6], 2), own, number, PB_DEV, N_DEV, K, CAP, 2))(route_owner_keys, route_owner_turns).reshape((BLOCKS, K))
    route_tile = with_ends(jax.random.randint(key_of[7], (BLOCKS, K), 0, NT_DEV), jax.random.fold_in(key_of[7], 1), 0, NT_DEV - 1).astype(jnp.int32)
    live_count = with_ends(jax.random.randint(key_of[8], (BLOCKS,), 3, K + 1), jax.random.fold_in(key_of[8], 1), 3, K).astype(jnp.int32)
    return dict(positions=positions, velocities=velocities, masses=masses, samples=samples, sample_mass=sample_mass, start_potential=start_potential, route_owner=route_owner, route_tile=route_tile, live_count=live_count)


EPSILON = 0.01
STIFFNESS = 150.0
TIMESTEP = 0.05
NEGATIVE = -1.0e30
HIGHEST = lax.Precision.HIGHEST


def pair_costs(block_coordinates, tile_coordinates):
    first = block_coordinates[0][None, :, None] - tile_coordinates[:, 0][:, None, :]
    second = block_coordinates[1][None, :, None] - tile_coordinates[:, 1][:, None, :]
    third = block_coordinates[2][None, :, None] - tile_coordinates[:, 2][:, None, :]
    return 0.5 * (first * first + second * second + third * third)


def row_lse(score, active_mask):
    masked = jnp.where(active_mask[:, None, None], score, NEGATIVE)
    top = jnp.max(masked, axis=(0, 2))
    total = jnp.sum(jnp.exp(masked - top[None, :, None]), axis=(0, 2))
    return top + jnp.log(total)


def transport_block_update(block_coordinates, logarithm_masses, tile_coordinates, tile_dual_values, active_mask):
    cost = pair_costs(block_coordinates, tile_coordinates)
    row_dual_values = EPSILON * logarithm_masses - EPSILON * row_lse((tile_dual_values[:, None, :] - cost) / EPSILON, active_mask)
    score = (row_dual_values[None, :, None] - cost) / EPSILON
    column_peak = jnp.max(score, axis=1)
    column_total_sum = jnp.sum(jnp.exp(score - column_peak[:, None, :]), axis=1)
    return row_dual_values, jnp.where(active_mask[:, None], column_peak, NEGATIVE), jnp.where(active_mask[:, None], column_total_sum, 0.0)


def centre_block(block_coordinates, tile_coordinates, tile_dual_values, active_mask):
    cost = pair_costs(block_coordinates, tile_coordinates)
    masked = jnp.where(active_mask[:, None, None], (tile_dual_values[:, None, :] - cost) / EPSILON, NEGATIVE)
    top = jnp.max(masked, axis=(0, 2))
    weight = jnp.exp(masked - top[None, :, None])
    total = jnp.sum(weight, axis=(0, 2))
    numer = jnp.einsum("kij,kdj->di", weight, tile_coordinates, precision=HIGHEST)
    return numer / total[None, :]


def reference(positions, velocities, masses, samples, sample_mass, start_potential, route_owner, route_tile, live_count):
    block_coordinates = positions.reshape(3, BLOCKS, BLK).transpose(1, 0, 2)
    logarithm_masses = jnp.log(masses).reshape(BLOCKS, BLK)
    tile_coordinates = samples.reshape(3, TILES, TILE).transpose(1, 0, 2)
    log_sample = jnp.log(sample_mass).reshape(TILES, TILE)
    tile_ids = (route_owner * NT_DEV + route_tile).astype(jnp.int32)
    active_mask = jnp.arange(K, dtype=jnp.int32)[None, :] < live_count[:, None]
    dual_variable = start_potential.reshape(TILES, TILE)
    for step in range(ITERS):
        def visit(carry, item, dual_variable=dual_variable):
            top_acc, sum_acc = carry
            point_coordinates, logarithm_weight, particle_labels, surviving_flags = item
            row_dual_values, column_peak, column_total_sum = transport_block_update(point_coordinates, logarithm_weight, tile_coordinates[particle_labels], dual_variable[particle_labels], surviving_flags)
            for slot in range(K):
                target = particle_labels[slot]
                old_top = top_acc[target]
                new_top = jnp.maximum(old_top, column_peak[slot])
                new_sum = sum_acc[target] * jnp.exp(old_top - new_top) + column_total_sum[slot] * jnp.exp(column_peak[slot] - new_top)
                top_acc = top_acc.at[target].set(new_top)
                sum_acc = sum_acc.at[target].set(new_sum)
            return (top_acc, sum_acc), None

        start = (jnp.full((TILES, TILE), NEGATIVE, jnp.float32), jnp.zeros((TILES, TILE), jnp.float32))
        (top_acc, sum_acc), unused = lax.scan(visit, start, (block_coordinates, logarithm_masses, tile_ids, active_mask))
        covered = sum_acc > 0
        updated = EPSILON * log_sample - EPSILON * (top_acc + jnp.log(jnp.where(covered, sum_acc, 1.0)))
        dual_variable = jnp.where(covered, updated, dual_variable)

    def centre_of(item):
        return centre_block(item[0], tile_coordinates[item[1]], dual_variable[item[1]], item[2])

    centres = lax.map(centre_of, (block_coordinates, tile_ids, active_mask))
    centre = centres.transpose(1, 0, 2).reshape(3, BLOCKS * BLK)
    new_velocity = velocities + STIFFNESS * (centre - positions)
    new_position = positions + TIMESTEP * new_velocity
    return new_position, new_velocity
```

```python
import math

import jax
import jax.numpy as jnp
from jax import lax
from jax.experimental import pallas as pl
from jax.experimental.pallas import tpu as pltpu
from jax.sharding import PartitionSpec as P

MESH = pl.DeviceIdType.MESH
F32, BF16 = jnp.float32, jnp.bfloat16

BLK = 128
TILE = 512
K = 4
ITERS = 2
DEVICES = 128
BLOCKS = 32
TILES = 64
SLOTS = 2 * DEVICES
GROUPS = 16
PEERS = 8

EPSILON = 0.01
STIFFNESS = 150.0
TIMESTEP = 0.05
SCALE = 1.0 / (EPSILON * math.log(2.0))
NEGATIVE = -1e30
ROW_LIFT = 8.0
COL_LIFT = 3.0


def turn(k):
    return k + k // 2 - 2 * (k // 3)


def coordinates(device):
    return device // 32, device // 8 % 4, device // 2 % 4, device % 2


def peer(me, code, sign):
    x, y, z, c = coordinates(me)
    dx, dy = turn(code // 32), turn(code // 8 % 4)
    dz, dc = turn(code // 2 % 4), code % 2
    x = (x + sign * dx + 4) % 4
    y = (y + sign * dy + 4) % 4
    z = (z + sign * dz + 4) % 4
    return x * 32 + y * 8 + z * 2 + (c + dc) % 2


def outer(a, b):
    return lax.dot_general(a, b, (((0,), (0,)), ((), ())), preferred_element_type=F32)


def inner(a, b):
    return lax.dot_general(a, b, (((1,), (0,)), ((), ())), preferred_element_type=F32)


def three(v):
    first = v.astype(BF16).astype(F32)
    rest = v - first
    second = rest.astype(BF16).astype(F32)
    return first, second, (rest - second).astype(BF16).astype(F32)


def kernel(
    block_of, slot_at, live, id_in, particles, log_mass, tiles, start, log_sample,
    centre,
    pos_out, pos_in, row_out, row_in, g_out, g_in, fin_out, fin_in,
    x_row, x_base, y_table, y_base, dual, u_parts, t_row,
    g_block, column, g_top, g_tile, parts, owner_mask,
    send, pos_sem, row_sem, g_sem, fin_sem,
):
    me = lax.axis_index("dev")
    barrier = pltpu.get_barrier_semaphore()

    def greet(q, c):
        pl.semaphore_signal(barrier, inc=1, device_id=(peer(me, q, 1),), device_id_type=MESH)
        return c

    lax.fori_loop(1, DEVICES, greet, 0)

    sub8 = lax.broadcasted_iota(jnp.int32, (8, 128), 0)
    low = sub8 < 4
    sub8w = lax.broadcasted_iota(jnp.int32, (8, TILE), 0)
    loww = sub8w < 4
    lane8 = lax.broadcasted_iota(jnp.int32, (8, 128), 1)
    sub64 = lax.broadcasted_iota(jnp.int32, (TILES, 128), 0)

    def stage_positions(q, c):
        pos_out[q] = jnp.concatenate(
            [particles[block_of[2 * q]], particles[block_of[2 * q + 1]]], axis=0
        )
        return c

    lax.fori_loop(0, DEVICES, stage_positions, 0)

    def build_tile(t, c):
        v = tiles[t]
        b1, b2, b3 = three(jnp.concatenate([v, v], axis=0))
        y_base[t, 0:8] = jnp.where(loww, b1, b2)
        y_base[t, 8:16] = jnp.where(sub8w == 7, 1.0, jnp.where(loww, b3, b1))
        third = jnp.where((sub8w == 3) | (sub8w == 7), 1.0, jnp.where(loww, b2, b3))
        y_table[t, 16:32] = jnp.concatenate([third, jnp.where(loww, b1, b2)], axis=0).astype(BF16)
        return c

    lax.fori_loop(0, TILES, build_tile, 0)

    def spread_dual():
        top = jnp.max(dual[...], axis=1, keepdims=True)
        for n, part in enumerate(three(dual[...] - top + ROW_LIFT)):
            u_parts[n] = part
        wide = jnp.broadcast_to(top, (TILES, 128))
        for t in range(TILES):
            t_row[t] = wide[t : t + 1] - ROW_LIFT

        def fill(i, c):
            at = pl.ds(pl.multiple_of(i * 8, 8), 8)
            u1, u2, u3 = u_parts[0, at], u_parts[1, at], u_parts[2, at]
            for j in range(8):
                t = i * 8 + j
                first = jnp.where(
                    sub8w == 3, u1[j : j + 1], jnp.where(sub8w == 7, u2[j : j + 1], y_base[t, 0:8])
                )
                second = jnp.where(sub8w == 3, u3[j : j + 1], y_base[t, 8:16])
                y_table[t, 0:16] = jnp.concatenate([first, second], axis=0).astype(BF16)
            return c

        lax.fori_loop(0, TILES // 8, fill, 0)

    dual[...] = start[...]
    spread_dual()
    g_block[BLOCKS] = jnp.full((1, 128), NEGATIVE, F32)

    pl.semaphore_wait(barrier, DEVICES - 1)

    def local(src, dst, sem):
        pltpu.make_async_copy(src, dst, sem).start()

    def remote(src, dst, out_sem, in_sem, device):
        pltpu.make_async_remote_copy(
            src_ref=src, dst_ref=dst, send_sem=out_sem, recv_sem=in_sem,
            device_id=(device,), device_id_type=MESH,
        ).start()

    def arrived(ref, sem):
        pltpu.make_async_copy(ref, ref, sem).wait()

    def eight(g):
        return pl.ds(g * PEERS, PEERS)

    def sixteen(g):
        return pl.ds(g * 2 * PEERS, 2 * PEERS)

    def pair(q):
        return pl.ds(2 * q, 2)

    local(pos_out.at[0], pos_in.at[0], pos_sem.at[0])

    def send_positions(q, c):
        to = peer(me, q, 1)
        remote(pos_out.at[q], pos_in.at[q], send.at[0], pos_sem.at[q // PEERS], to)
        return c

    lax.fori_loop(1, DEVICES, send_positions, 0)

    def build_x(q):
        a = three(pos_in[q])
        r = [pltpu.roll(v, 4, 0) for v in a]
        for n, (lo, hi) in enumerate(((a, r), (r, a))):
            quarters = (
                jnp.where(low, lo[0], hi[0]), jnp.where(low, lo[0], hi[1]),
                jnp.where(low, lo[1], hi[1]), jnp.where(low, lo[2], hi[2]),
            )
            base = jnp.concatenate(quarters, axis=0)
            x_base[2 * q + n] = base
            ones = (
                jnp.where((sub8 == 3) | (sub8 == 7), 1.0, quarters[0]),
                jnp.where(sub8 == 3, 1.0, quarters[1]),
            )
            x_row[2 * q + n] = jnp.concatenate(ones + quarters[2:], axis=0).astype(BF16)

    def return_pairs(g, out, into, out_sem, in_sem):
        for j in range(PEERS):
            q = g * PEERS + j
            back = peer(me, q, -1)
            if j == 0:

                @pl.when(g == 0)
                def _():
                    local(out.at[pair(q)], into.at[pair(q)], in_sem.at[g])

                @pl.when(g > 0)
                def _():
                    remote(out.at[pair(q)], into.at[pair(q)], out_sem, in_sem.at[g], back)
            else:
                remote(out.at[pair(q)], into.at[pair(q)], out_sem, in_sem.at[g], back)

    def tile_id(g, n):
        return id_in[g * 2 * PEERS + n]

    def row_pass(step):
        def body(g, c):
            if step == 0:
                arrived(pos_in.at[eight(g)], pos_sem.at[g])
                for j in range(PEERS):
                    build_x(g * PEERS + j)
            for n in range(2 * PEERS):
                s = g * 2 * PEERS + n
                t = tile_id(g, n)
                e = outer(y_table[t], x_row[s])
                total = jnp.sum(jnp.exp2(e), axis=0, keepdims=True)
                row_out[step, s] = t_row[t] + jnp.log2(total)
            return_pairs(g, row_out.at[step], row_in.at[step], send.at[1 + step], row_sem.at[step])
            return c

        lax.fori_loop(0, GROUPS, body, 0)

    def particle_side(step):
        for g in range(GROUPS):
            arrived(row_in.at[step, sixteen(g)], row_sem.at[step, g])

        def of_block(b, c):
            row = [row_in[step, slot_at[K * b + k]] for k in range(K)]
            row = [jnp.where(k < live[b], v, NEGATIVE) for k, v in enumerate(row)]
            top = jnp.maximum(jnp.maximum(row[0], row[1]), jnp.maximum(row[2], row[3]))
            total = sum(jnp.exp2(v - top) for v in row)
            g_block[b] = log_mass[b] - (top + jnp.log2(total))
            return c

        lax.fori_loop(0, BLOCKS, of_block, 0)

        def send_g(q, c):
            g_out[step, 2 * q] = g_block[block_of[2 * q]]
            g_out[step, 2 * q + 1] = g_block[block_of[2 * q + 1]]

            @pl.when(q == 0)
            def _():
                local(g_out.at[step, pair(q)], g_in.at[step, pair(q)], g_sem.at[step, q // PEERS])

            @pl.when(q > 0)
            def _():
                remote(
                    g_out.at[step, pair(q)], g_in.at[step, pair(q)], send.at[3 + step],
                    g_sem.at[step, q // PEERS], peer(me, q, 1),
                )
            return c

        lax.fori_loop(0, DEVICES, send_g, 0)

    def column_pass(step):
        def body(g, best):
            arrived(g_in.at[step, sixteen(g)], g_sem.at[step, g])
            for half in range(2):
                at = pl.ds(pl.multiple_of(g * 16 + half * 8, 8), 8)
                values = g_in[step, at].reshape(8, 128)
                top = jnp.max(values, axis=1, keepdims=True)
                g1, g2, g3 = three(values - top + COL_LIFT)
                g_top[at] = jnp.broadcast_to(top, (8, 128))
                sums = []
                for j in range(8):
                    n = half * 8 + j
                    s = g * 16 + n
                    t = tile_id(g, n)
                    second = jnp.where(sub8 == 7, g1[j : j + 1], x_base[s, 8:16])
                    third = jnp.where(
                        sub8 == 3, g2[j : j + 1], jnp.where(sub8 == 7, g3[j : j + 1], x_base[s, 16:24])
                    )
                    x = jnp.concatenate([x_base[s, 0:8], second, third, x_base[s, 24:32]], axis=0)
                    e = outer(x.astype(BF16), y_table[t])
                    sums.append(jnp.sum(jnp.exp2(e), axis=0, keepdims=True))
                    best = jnp.maximum(best, jnp.where(sub64 == t, values[j : j + 1], NEGATIVE))
                column[at] = jnp.concatenate(sums, axis=0)
            return best

        best = lax.fori_loop(0, GROUPS, body, jnp.full((TILES, 128), NEGATIVE, F32))
        level = jnp.max(best, axis=1, keepdims=True)
        wide = jnp.broadcast_to(level, (TILES, 128))
        for t in range(TILES):
            g_tile[t] = wide[t : t + 1]

        def scale(g, c):
            part, mask = [], []
            for half in range(2):
                at = pl.ds(pl.multiple_of(g * 16 + half * 8, 8), 8)
                names = [tile_id(g, half * 8 + j) for j in range(8)]
                tops = jnp.concatenate([g_tile[t] for t in names], axis=0)
                factor = jnp.exp2(0.5 * (g_top[at] - tops))
                factor = jnp.concatenate([factor] * 4, axis=1)
                part.append(three(column[at] * factor * factor))
                name = jnp.full((8, 128), names[0], jnp.int32)
                for j in range(1, 8):
                    name = jnp.where(sub8 == j, names[j], name)
                mask.append(jnp.where(name == lane8, 1.0, 0.0))
            at = pl.ds(pl.multiple_of(g * 16, 16), 16)
            for n in range(3):
                parts[n, at] = jnp.concatenate([part[0][n], part[1][n]], axis=0).astype(BF16)
            owner_mask[at] = jnp.concatenate(mask, axis=0).astype(BF16)
            return c

        lax.fori_loop(0, GROUPS, scale, 0)
        total = sum(outer(owner_mask[...], parts[n]) for n in range(3))[0:TILES]
        covered = level > 0.1 * NEGATIVE
        updated = log_sample[...] - (level - COL_LIFT + jnp.log2(jnp.where(covered, total, 1.0)))
        dual[...] = jnp.where(covered, updated, dual[...])
        spread_dual()

    for step in range(ITERS):
        row_pass(step)
        particle_side(step)
        column_pass(step)

    sub4 = lax.broadcasted_iota(jnp.int32, (4, 128), 0)

    def final(g, c):
        for n in range(2 * PEERS):
            s = g * 2 * PEERS + n
            t = tile_id(g, n)
            y = y_table[t]
            weight = jnp.exp2(outer(y, x_row[s]))
            coarse = weight.astype(BF16)
            fine = (weight - coarse.astype(F32)).astype(BF16)
            sums = inner(y, coarse) + inner(y, fine)
            mass = sums[15:16]
            where = sums[0:4] + sums[4:8] + sums[8:12]
            fin_out[s] = jnp.where(sub4 == 3, t_row[t] + jnp.log2(mass), where / mass)
        return_pairs(g, fin_out, fin_in, send.at[5], fin_sem)
        return c

    lax.fori_loop(0, GROUPS, final, 0)
    for g in range(GROUPS):
        arrived(fin_in.at[sixteen(g)], fin_sem.at[g])

    def finish(b, c):
        got = [fin_in[slot_at[K * b + k]] for k in range(K)]
        row = [jnp.where(k < live[b], v[3:4], NEGATIVE) for k, v in enumerate(got)]
        top = jnp.maximum(jnp.maximum(row[0], row[1]), jnp.maximum(row[2], row[3]))
        weight = [jnp.exp2(v - top) for v in row]
        total = weight[0] + weight[1] + weight[2] + weight[3]
        centre[b] = sum(w * v for w, v in zip(weight, got)) / total
        return c

    lax.fori_loop(0, BLOCKS, finish, 0)

    most = pl.ds(0, DEVICES - 1)
    rows = pl.ds(0, 2 * (DEVICES - 1))
    arrived(pos_out.at[most], send.at[0])
    for step in range(ITERS):
        arrived(row_out.at[step, rows], send.at[1 + step])
        arrived(g_out.at[step, rows], send.at[3 + step])
    arrived(fin_out.at[rows], send.at[5])


def local_step(
    positions, velocities, masses, samples, sample_mass, start_potential,
    route_owner, route_tile, live_count,
):
    me = lax.axis_index("dev")
    slots = BLOCKS * K
    owner = route_owner.reshape(slots)
    x, y, z, c = coordinates(me)
    ox, oy, oz, oc = coordinates(owner)
    code = (
        turn((ox - x + 4) % 4) * 32 + turn((oy - y + 4) % 4) * 8
        + turn((oz - z + 4) % 4) * 2 + (oc - c + 2) % 2
    )
    number = jnp.arange(slots, dtype=jnp.int32)
    alive = (jnp.arange(K, dtype=jnp.int32)[None, :] < live_count[:, None]).reshape(slots)
    same = (code[:, None] == code[None, :]) & alive[:, None] & (number[:, None] < number[None, :])
    place = 2 * code + jnp.sum(same.astype(jnp.int32), axis=0)
    slot_at = jnp.where(alive, place, 0)
    here = (jnp.arange(SLOTS, dtype=jnp.int32)[:, None] == place[None, :]) & alive[None, :]
    block_of = BLOCKS - jnp.sum(jnp.where(here, BLOCKS - number // K, 0), axis=1)
    named = jnp.sum(jnp.where(here, route_tile.reshape(slots)[None, :], 0), axis=1)
    device = jnp.arange(DEVICES, dtype=jnp.int32)
    dx, dy, dz, dc = coordinates(device)
    code_of = (
        turn((dx - x + 4) % 4) * 32 + turn((dy - y + 4) % 4) * 8
        + turn((dz - z + 4) % 4) * 2 + (dc - c + 2) % 2
    )
    asked = lax.all_to_all(
        named.reshape(DEVICES, 2)[code_of], "dev", split_axis=0, concat_axis=0, tiled=True
    )
    ids = asked[peer(me, device, -1)].reshape(SLOTS)

    by_block = positions.reshape(3, BLOCKS, BLK).transpose(1, 0, 2)
    particles = jnp.pad(SCALE * (by_block - 0.5), ((0, 1), (0, 1), (0, 0)))
    log_mass = jnp.log2(masses).reshape(BLOCKS, 1, BLK)
    shifted = samples - 0.5
    tiles = jnp.pad(
        shifted.reshape(3, TILES, TILE).transpose(1, 0, 2), ((0, 0), (0, 1), (0, 0))
    )
    start = SCALE * (start_potential - 0.5 * jnp.sum(shifted * shifted, axis=0))
    log_sample = jnp.log2(sample_mass).reshape(TILES, TILE)

    vmem, smem = pl.BlockSpec(memory_space=pltpu.VMEM), pl.BlockSpec(memory_space=pltpu.SMEM)
    dma = pltpu.SemaphoreType.DMA
    centre = pl.pallas_call(
        kernel,
        out_shape=jax.ShapeDtypeStruct((BLOCKS, 4, BLK), F32),
        in_specs=[smem] * 4 + [vmem] * 5,
        out_specs=vmem,
        scratch_shapes=[
            pltpu.VMEM((DEVICES, 8, 128), F32),
            pltpu.VMEM((DEVICES, 8, 128), F32),
            pltpu.VMEM((ITERS, SLOTS, 1, 128), F32),
            pltpu.VMEM((ITERS, SLOTS, 1, 128), F32),
            pltpu.VMEM((ITERS, SLOTS, 1, 128), F32),
            pltpu.VMEM((ITERS, SLOTS, 1, 128), F32),
            pltpu.VMEM((SLOTS, 4, 128), F32),
            pltpu.VMEM((SLOTS, 4, 128), F32),
            pltpu.VMEM((SLOTS, 32, 128), BF16),
            pltpu.VMEM((SLOTS, 32, 128), F32),
            pltpu.VMEM((TILES, 32, TILE), BF16),
            pltpu.VMEM((TILES, 16, TILE), F32),
            pltpu.VMEM((TILES, TILE), F32),
            pltpu.VMEM((3, TILES, TILE), F32),
            pltpu.VMEM((TILES, 1, 128), F32),
            pltpu.VMEM((BLOCKS + 1, 1, 128), F32),
            pltpu.VMEM((SLOTS, TILE), F32),
            pltpu.VMEM((SLOTS, 128), F32),
            pltpu.VMEM((TILES, 1, 128), F32),
            pltpu.VMEM((3, SLOTS, TILE), BF16),
            pltpu.VMEM((SLOTS, 128), BF16),
            dma((6,)),
            dma((GROUPS,)),
            dma((ITERS, GROUPS)),
            dma((ITERS, GROUPS)),
            dma((GROUPS,)),
        ],
        compiler_params=pltpu.CompilerParams(
            collective_id=0, has_side_effects=True, vmem_limit_bytes=48 << 20
        ),
        cost_estimate=pl.CostEstimate(
            flops=5 * 64 * SLOTS * BLK * TILE,
            transcendentals=5 * SLOTS * BLK * TILE,
            bytes_accessed=2 << 20,
        ),
    )(block_of, slot_at, live_count, ids, particles, log_mass, tiles, start.reshape(TILES, TILE), log_sample)

    middle = centre[:, 0:3].transpose(1, 0, 2).reshape(3, BLOCKS * BLK) + 0.5
    new_velocity = velocities + STIFFNESS * (middle - positions)
    return positions + TIMESTEP * new_velocity, new_velocity


def solution(mesh):
    across, along = P(None, "dev"), P("dev")
    return jax.shard_map(
        local_step,
        mesh=mesh,
        in_specs=(
            across, across, along, across, along, along, P("dev", None), P("dev", None), along
        ),
        out_specs=(across, across),
        check_vma=False,
    )
```

```python
import math

import jax
import jax.numpy as jnp
from jax import lax
from jax.experimental import pallas as pl
from jax.experimental.pallas import tpu as pltpu
from jax.sharding import PartitionSpec as P

MESH = pl.DeviceIdType.MESH
F32, BF16 = jnp.float32, jnp.bfloat16

BLK = 128
TILE = 512
K = 4
ITERS = 2
DEVICES = 128
BLOCKS = 32
TILES = 64
SLOTS = 2 * DEVICES
GROUPS = 16
PEERS = 8

EPSILON = 0.01
STIFFNESS = 150.0
TIMESTEP = 0.05
SCALE = 1.0 / (EPSILON * math.log(2.0))
NEGATIVE = -1e30
ROW_LIFT = 8.0
COL_LIFT = 3.0


def outer(a, b):
    return lax.dot_general(a, b, (((0,), (0,)), ((), ())), preferred_element_type=F32)


def inner(a, b):
    return lax.dot_general(a, b, (((1,), (0,)), ((), ())), preferred_element_type=F32)


def three(v):
    first = v.astype(BF16).astype(F32)
    rest = v - first
    second = rest.astype(BF16).astype(F32)
    return first, second, (rest - second).astype(BF16).astype(F32)


def kernel(
    block_of, slot_at, live, ids, particles, log_mass, tiles, start, log_sample,
    centre,
    pos_out, pos_in, id_in, names, row_out, row_in, g_out, g_in, fin_out, fin_in,
    x_row, x_base, y_table, y_base, dual, u_parts, t_row,
    g_block, column, g_top, g_tile, parts, owner_mask,
    send, pos_sem, id_sem, row_sem, g_sem, fin_sem,
):
    me = lax.axis_index("dev")
    barrier = pltpu.get_barrier_semaphore()

    def greet(q, c):
        pl.semaphore_signal(barrier, inc=1, device_id=(me ^ q,), device_id_type=MESH)
        return c

    lax.fori_loop(1, DEVICES, greet, 0)

    sub8 = lax.broadcasted_iota(jnp.int32, (8, 128), 0)
    low = sub8 < 4
    sub8w = lax.broadcasted_iota(jnp.int32, (8, TILE), 0)
    loww = sub8w < 4
    lane8 = lax.broadcasted_iota(jnp.int32, (8, 128), 1)
    sub64 = lax.broadcasted_iota(jnp.int32, (TILES, 128), 0)

    def stage_positions(g, c):
        for j in range(PEERS):
            q = g * PEERS + j
            pos_out[q] = jnp.concatenate(
                [particles[block_of[2 * q]], particles[block_of[2 * q + 1]]], axis=0
            )
        return c

    lax.fori_loop(0, GROUPS, stage_positions, 0)

    def build_tile(t, c):
        v = tiles[t]
        b1, b2, b3 = three(jnp.concatenate([v, v], axis=0))
        y_base[t, 0:8] = jnp.where(loww, b1, b2)
        y_base[t, 8:16] = jnp.where(sub8w == 7, 1.0, jnp.where(loww, b3, b1))
        third = jnp.where((sub8w == 3) | (sub8w == 7), 1.0, jnp.where(loww, b2, b3))
        y_table[t, 16:32] = jnp.concatenate([third, jnp.where(loww, b1, b2)], axis=0).astype(BF16)
        return c

    lax.fori_loop(0, TILES, build_tile, 0)

    def spread_dual():
        top = jnp.max(dual[...], axis=1, keepdims=True)
        for n, part in enumerate(three(dual[...] - top + ROW_LIFT)):
            u_parts[n] = part
        wide = jnp.broadcast_to(top, (TILES, 128))
        for t in range(TILES):
            t_row[t] = wide[t : t + 1] - ROW_LIFT

        def fill(i, c):
            at = pl.ds(pl.multiple_of(i * 8, 8), 8)
            u1, u2, u3 = u_parts[0, at], u_parts[1, at], u_parts[2, at]
            for j in range(8):
                t = i * 8 + j
                first = jnp.where(
                    sub8w == 3, u1[j : j + 1], jnp.where(sub8w == 7, u2[j : j + 1], y_base[t, 0:8])
                )
                second = jnp.where(sub8w == 3, u3[j : j + 1], y_base[t, 8:16])
                y_table[t, 0:16] = jnp.concatenate([first, second], axis=0).astype(BF16)
            return c

        lax.fori_loop(0, TILES // 8, fill, 0)

    dual[...] = start[...]
    spread_dual()
    g_block[BLOCKS] = jnp.full((1, 128), NEGATIVE, F32)

    pl.semaphore_wait(barrier, DEVICES - 1)

    def local(src, dst, sem):
        pltpu.make_async_copy(src, dst, sem).start()

    def remote(src, dst, out_sem, in_sem, device):
        pltpu.make_async_remote_copy(
            src_ref=src, dst_ref=dst, send_sem=out_sem, recv_sem=in_sem,
            device_id=(device,), device_id_type=MESH,
        ).start()

    def arrived(ref, sem):
        pltpu.make_async_copy(ref, ref, sem).wait()

    def eight(g):
        return pl.ds(g * PEERS, PEERS)

    def sixteen(g):
        return pl.ds(g * 2 * PEERS, 2 * PEERS)

    def pair(q):
        return pl.ds(2 * q, 2)

    def exchange(g, sends):
        for j in range(PEERS):
            q = g * PEERS + j
            for out, into, out_sem, in_sem in sends(q):
                if j == 0:

                    @pl.when(g == 0)
                    def _():
                        local(out, into, in_sem)

                    @pl.when(g > 0)
                    def _():
                        remote(out, into, out_sem, in_sem, me ^ q)
                else:
                    remote(out, into, out_sem, in_sem, me ^ q)

    def send_positions(g, c):
        exchange(
            g,
            lambda q: (
                (ids.at[pair(q)], id_in.at[pair(q)], send.at[6], id_sem.at[g]),
                (pos_out.at[q], pos_in.at[q], send.at[0], pos_sem.at[g]),
            ),
        )
        return c

    lax.fori_loop(0, GROUPS, send_positions, 0)

    def build_x(q):
        a = three(pos_in[q])
        r = [pltpu.roll(v, 4, 0) for v in a]
        for n, (lo, hi) in enumerate(((a, r), (r, a))):
            quarters = (
                jnp.where(low, lo[0], hi[0]), jnp.where(low, lo[0], hi[1]),
                jnp.where(low, lo[1], hi[1]), jnp.where(low, lo[2], hi[2]),
            )
            base = jnp.concatenate(quarters, axis=0)
            x_base[2 * q + n] = base
            ones = (
                jnp.where((sub8 == 3) | (sub8 == 7), 1.0, quarters[0]),
                jnp.where(sub8 == 3, 1.0, quarters[1]),
            )
            x_row[2 * q + n] = jnp.concatenate(ones + quarters[2:], axis=0).astype(BF16)

    def return_pairs(g, out, into, out_sem, in_sem):
        exchange(g, lambda q: ((out.at[pair(q)], into.at[pair(q)], out_sem, in_sem.at[g]),))

    def tile_id(g, n):
        return names[g * 2 * PEERS + n]

    def row_pass(step):
        def body(g, c):
            if step == 0:
                arrived(id_in.at[sixteen(g)], id_sem.at[g])
                for n in range(2 * PEERS):
                    names[g * 2 * PEERS + n] = id_in[g * 2 * PEERS + n][0, 0]
                arrived(pos_in.at[eight(g)], pos_sem.at[g])
                for j in range(PEERS):
                    build_x(g * PEERS + j)
            for n in range(2 * PEERS):
                s = g * 2 * PEERS + n
                t = tile_id(g, n)
                e = outer(y_table[t], x_row[s])
                total = jnp.sum(jnp.exp2(e), axis=0, keepdims=True)
                row_out[step, s] = t_row[t] + jnp.log2(total)
            return_pairs(g, row_out.at[step], row_in.at[step], send.at[1 + step], row_sem.at[step])
            return c

        lax.fori_loop(0, GROUPS, body, 0)

    def particle_side(step):
        for g in range(GROUPS):
            arrived(row_in.at[step, sixteen(g)], row_sem.at[step, g])

        def of_blocks(i, c):
            for j in range(8):
                b = i * 8 + j
                row = [row_in[step, slot_at[K * b + k]] for k in range(K)]
                row = [jnp.where(k < live[b], v, NEGATIVE) for k, v in enumerate(row)]
                top = jnp.maximum(jnp.maximum(row[0], row[1]), jnp.maximum(row[2], row[3]))
                total = sum(jnp.exp2(v - top) for v in row)
                g_block[b] = log_mass[b] - (top + jnp.log2(total))
            return c

        lax.fori_loop(0, BLOCKS // 8, of_blocks, 0)

        def send_g(g, c):
            for n in range(2 * PEERS):
                s = g * 2 * PEERS + n
                g_out[step, s] = g_block[block_of[s]]
            return_pairs(g, g_out.at[step], g_in.at[step], send.at[3 + step], g_sem.at[step])
            return c

        lax.fori_loop(0, GROUPS, send_g, 0)

    def column_pass(step):
        def body(g, best):
            arrived(g_in.at[step, sixteen(g)], g_sem.at[step, g])
            for half in range(2):
                at = pl.ds(pl.multiple_of(g * 16 + half * 8, 8), 8)
                values = g_in[step, at].reshape(8, 128)
                top = jnp.max(values, axis=1, keepdims=True)
                g1, g2, g3 = three(values - top + COL_LIFT)
                g_top[at] = jnp.broadcast_to(top, (8, 128))
                sums = []
                for j in range(8):
                    n = half * 8 + j
                    s = g * 16 + n
                    t = tile_id(g, n)
                    second = jnp.where(sub8 == 7, g1[j : j + 1], x_base[s, 8:16])
                    third = jnp.where(
                        sub8 == 3, g2[j : j + 1], jnp.where(sub8 == 7, g3[j : j + 1], x_base[s, 16:24])
                    )
                    x = jnp.concatenate([x_base[s, 0:8], second, third, x_base[s, 24:32]], axis=0)
                    e = outer(x.astype(BF16), y_table[t])
                    sums.append(jnp.sum(jnp.exp2(e), axis=0, keepdims=True))
                    best = jnp.maximum(best, jnp.where(sub64 == t, values[j : j + 1], NEGATIVE))
                column[at] = jnp.concatenate(sums, axis=0)
            return best

        best = lax.fori_loop(0, GROUPS, body, jnp.full((TILES, 128), NEGATIVE, F32))
        level = jnp.max(best, axis=1, keepdims=True)
        wide = jnp.broadcast_to(level, (TILES, 128))
        for t in range(TILES):
            g_tile[t] = wide[t : t + 1]

        def scale(g, c):
            part, mask = [], []
            for half in range(2):
                at = pl.ds(pl.multiple_of(g * 16 + half * 8, 8), 8)
                named = [tile_id(g, half * 8 + j) for j in range(8)]
                tops = jnp.concatenate([g_tile[t] for t in named], axis=0)
                factor = jnp.exp2(0.5 * (g_top[at] - tops))
                factor = jnp.concatenate([factor] * 4, axis=1)
                part.append(three(column[at] * factor * factor))
                name = jnp.full((8, 128), named[0], jnp.int32)
                for j in range(1, 8):
                    name = jnp.where(sub8 == j, named[j], name)
                mask.append(jnp.where(name == lane8, 1.0, 0.0))
            at = pl.ds(pl.multiple_of(g * 16, 16), 16)
            for n in range(3):
                parts[n, at] = jnp.concatenate([part[0][n], part[1][n]], axis=0).astype(BF16)
            owner_mask[at] = jnp.concatenate(mask, axis=0).astype(BF16)
            return c

        lax.fori_loop(0, GROUPS, scale, 0)
        total = sum(outer(owner_mask[...], parts[n]) for n in range(3))[0:TILES]
        covered = level > 0.1 * NEGATIVE
        updated = log_sample[...] - (level - COL_LIFT + jnp.log2(jnp.where(covered, total, 1.0)))
        dual[...] = jnp.where(covered, updated, dual[...])
        spread_dual()

    for step in range(ITERS):
        row_pass(step)
        particle_side(step)
        column_pass(step)

    sub4 = lax.broadcasted_iota(jnp.int32, (4, 128), 0)

    def final(g, c):
        for n in range(2 * PEERS):
            s = g * 2 * PEERS + n
            t = tile_id(g, n)
            y = y_table[t]
            weight = jnp.exp2(outer(y, x_row[s]))
            coarse = weight.astype(BF16)
            fine = (weight - coarse.astype(F32)).astype(BF16)
            sums = inner(y, coarse) + inner(y, fine)
            mass = sums[15:16]
            where = sums[0:4] + sums[4:8] + sums[8:12]
            fin_out[s] = jnp.where(sub4 == 3, t_row[t] + jnp.log2(mass), where / mass)
        return_pairs(g, fin_out, fin_in, send.at[5], fin_sem)
        return c

    lax.fori_loop(0, GROUPS, final, 0)
    for g in range(GROUPS):
        arrived(fin_in.at[sixteen(g)], fin_sem.at[g])

    def finish(i, c):
        for j in range(8):
            b = i * 8 + j
            got = [fin_in[slot_at[K * b + k]] for k in range(K)]
            row = [jnp.where(k < live[b], v[3:4], NEGATIVE) for k, v in enumerate(got)]
            top = jnp.maximum(jnp.maximum(row[0], row[1]), jnp.maximum(row[2], row[3]))
            weight = [jnp.exp2(v - top) for v in row]
            total = weight[0] + weight[1] + weight[2] + weight[3]
            centre[b] = sum(w * v for w, v in zip(weight, got)) / total
        return c

    lax.fori_loop(0, BLOCKS // 8, finish, 0)

    most = pl.ds(0, DEVICES - 1)
    rows = pl.ds(0, 2 * (DEVICES - 1))
    arrived(pos_out.at[most], send.at[0])
    arrived(ids.at[rows], send.at[6])
    for step in range(ITERS):
        arrived(row_out.at[step, rows], send.at[1 + step])
        arrived(g_out.at[step, rows], send.at[3 + step])
    arrived(fin_out.at[rows], send.at[5])


def local_step(
    positions, velocities, masses, samples, sample_mass, start_potential,
    route_owner, route_tile, live_count,
):
    me = lax.axis_index("dev")
    slots = BLOCKS * K
    owner = route_owner.reshape(slots)
    code = owner ^ me
    number = jnp.arange(slots, dtype=jnp.int32)
    alive = (jnp.arange(K, dtype=jnp.int32)[None, :] < live_count[:, None]).reshape(slots)
    same = (code[:, None] == code[None, :]) & alive[:, None] & (number[:, None] < number[None, :])
    place = 2 * code + jnp.sum(same.astype(jnp.int32), axis=0)
    slot_at = jnp.where(alive, place, 0)
    here = (jnp.arange(SLOTS, dtype=jnp.int32)[:, None] == place[None, :]) & alive[None, :]
    block_of = BLOCKS - jnp.sum(jnp.where(here, BLOCKS - number // K, 0), axis=1)
    named = jnp.sum(jnp.where(here, route_tile.reshape(slots)[None, :], 0), axis=1)
    ids = jnp.broadcast_to(named[:, None, None], (SLOTS, 1, 128))

    by_block = positions.reshape(3, BLOCKS, BLK).transpose(1, 0, 2)
    particles = jnp.pad(SCALE * (by_block - 0.5), ((0, 1), (0, 1), (0, 0)))
    log_mass = jnp.log2(masses).reshape(BLOCKS, 1, BLK)
    shifted = samples - 0.5
    tiles = jnp.pad(
        shifted.reshape(3, TILES, TILE).transpose(1, 0, 2), ((0, 0), (0, 1), (0, 0))
    )
    start = SCALE * (start_potential - 0.5 * jnp.sum(shifted * shifted, axis=0))
    log_sample = jnp.log2(sample_mass).reshape(TILES, TILE)

    vmem, smem = pl.BlockSpec(memory_space=pltpu.VMEM), pl.BlockSpec(memory_space=pltpu.SMEM)
    dma = pltpu.SemaphoreType.DMA
    centre = pl.pallas_call(
        kernel,
        out_shape=jax.ShapeDtypeStruct((BLOCKS, 4, BLK), F32),
        in_specs=[smem] * 3 + [vmem] * 6,
        out_specs=vmem,
        scratch_shapes=[
            pltpu.VMEM((DEVICES, 8, 128), F32),
            pltpu.VMEM((DEVICES, 8, 128), F32),
            pltpu.VMEM((SLOTS, 1, 128), jnp.int32),
            pltpu.SMEM((SLOTS,), jnp.int32),
            pltpu.VMEM((ITERS, SLOTS, 1, 128), F32),
            pltpu.VMEM((ITERS, SLOTS, 1, 128), F32),
            pltpu.VMEM((ITERS, SLOTS, 1, 128), F32),
            pltpu.VMEM((ITERS, SLOTS, 1, 128), F32),
            pltpu.VMEM((SLOTS, 4, 128), F32),
            pltpu.VMEM((SLOTS, 4, 128), F32),
            pltpu.VMEM((SLOTS, 32, 128), BF16),
            pltpu.VMEM((SLOTS, 32, 128), F32),
            pltpu.VMEM((TILES, 32, TILE), BF16),
            pltpu.VMEM((TILES, 16, TILE), F32),
            pltpu.VMEM((TILES, TILE), F32),
            pltpu.VMEM((3, TILES, TILE), F32),
            pltpu.VMEM((TILES, 1, 128), F32),
            pltpu.VMEM((BLOCKS + 1, 1, 128), F32),
            pltpu.VMEM((SLOTS, TILE), F32),
            pltpu.VMEM((SLOTS, 128), F32),
            pltpu.VMEM((TILES, 1, 128), F32),
            pltpu.VMEM((3, SLOTS, TILE), BF16),
            pltpu.VMEM((SLOTS, 128), BF16),
            dma((7,)),
            dma((GROUPS,)),
            dma((GROUPS,)),
            dma((ITERS, GROUPS)),
            dma((ITERS, GROUPS)),
            dma((GROUPS,)),
        ],
        compiler_params=pltpu.CompilerParams(
            collective_id=0, has_side_effects=True, vmem_limit_bytes=48 << 20
        ),
        cost_estimate=pl.CostEstimate(
            flops=5 * 64 * SLOTS * BLK * TILE,
            transcendentals=5 * SLOTS * BLK * TILE,
            bytes_accessed=2 << 20,
        ),
    )(block_of, slot_at, live_count, ids, particles, log_mass, tiles, start.reshape(TILES, TILE), log_sample)

    middle = centre[:, 0:3].transpose(1, 0, 2).reshape(3, BLOCKS * BLK) + 0.5
    new_velocity = velocities + STIFFNESS * (middle - positions)
    return positions + TIMESTEP * new_velocity, new_velocity


def solution(mesh):
    across, along = P(None, "dev"), P("dev")
    return jax.shard_map(
        local_step,
        mesh=mesh,
        in_specs=(
            across, across, along, across, along, along, P("dev", None), P("dev", None), along
        ),
        out_specs=(across, across),
        check_vma=False,
    )
```

```python
import math

import jax
import jax.numpy as jnp
from jax import lax
from jax.experimental import pallas as pl
from jax.experimental.pallas import tpu as pltpu
from jax.sharding import PartitionSpec as P

MESH = pl.DeviceIdType.MESH
F32, BF16 = jnp.float32, jnp.bfloat16

BLK = 128
TILE = 512
K = 4
ITERS = 2
DEVICES = 128
BLOCKS = 32
TILES = 64
SLOTS = 2 * DEVICES
GROUPS = 8
PEERS = 16
WIDTH = 2 * PEERS

EPSILON = 0.01
STIFFNESS = 150.0
TIMESTEP = 0.05
SCALE = 1.0 / (EPSILON * math.log(2.0))
NEGATIVE = -1e30
ROW_LIFT = 8.0
COL_LIFT = 3.0


def outer(a, b):
    return lax.dot_general(a, b, (((0,), (0,)), ((), ())), preferred_element_type=F32)


def inner(a, b):
    return lax.dot_general(a, b, (((1,), (0,)), ((), ())), preferred_element_type=F32)


def three(v):
    first = v.astype(BF16).astype(F32)
    rest = v - first
    second = rest.astype(BF16).astype(F32)
    return first, second, (rest - second).astype(BF16).astype(F32)


def kernel(
    block_of, slot_at, live, ids, particles, masses, tiles, start, sample_mass,
    centre,
    pos_out, pos_in, id_in, names, row_out, row_in, g_out, g_in, fin_out, fin_in,
    x_row, x_base, y_table, y_base, dual, u_parts, t_row,
    log_sample, g_block, column, g_top, g_tile, parts, owner_mask,
    send, pos_sem, id_sem, row_sem, g_sem, fin_sem,
):
    me = lax.axis_index("dev")
    barrier = pltpu.get_barrier_semaphore()

    def greet(q, c):
        pl.semaphore_signal(barrier, inc=1, device_id=(me ^ q,), device_id_type=MESH)
        return c

    lax.fori_loop(1, DEVICES, greet, 0)

    sub8 = lax.broadcasted_iota(jnp.int32, (8, 128), 0)
    low = sub8 < 4
    sub8w = lax.broadcasted_iota(jnp.int32, (8, TILE), 0)
    loww = sub8w < 4
    lane8 = lax.broadcasted_iota(jnp.int32, (8, 128), 1)
    sub64 = lax.broadcasted_iota(jnp.int32, (TILES, 128), 0)

    blank = jnp.zeros((1, 128), F32)
    blankw = jnp.zeros((1, TILE), F32)

    def stage_positions(g, c):
        for j in range(PEERS):
            q = g * PEERS + j
            first, second = (
                particles[jnp.minimum(block_of[2 * q + n], BLOCKS - 1)] for n in range(2)
            )
            pos_out[q] = jnp.concatenate([first, blank, second, blank], axis=0)
        return c

    lax.fori_loop(0, GROUPS, stage_positions, 0)

    def build_tiles(i, c):
        duals, logs = [], []
        for j in range(8):
            t = i * 8 + j
            v = tiles[t] - 0.5
            duals.append(start[t] - 0.5 * jnp.sum(v * v, axis=0, keepdims=True))
            logs.append(sample_mass[t])
            b1, b2, b3 = three(jnp.concatenate([v, blankw, v, blankw], axis=0))
            y_base[t, 0:8] = jnp.where(loww, b1, b2)
            y_base[t, 8:16] = jnp.where(sub8w == 7, 1.0, jnp.where(loww, b3, b1))
            third = jnp.where((sub8w == 3) | (sub8w == 7), 1.0, jnp.where(loww, b2, b3))
            y_table[t, 16:32] = jnp.concatenate(
                [third, jnp.where(loww, b1, b2)], axis=0
            ).astype(BF16)
        at = pl.ds(pl.multiple_of(i * 8, 8), 8)
        dual[at] = SCALE * jnp.concatenate(duals, axis=0)
        log_sample[at] = jnp.log2(jnp.concatenate(logs, axis=0))
        return c

    lax.fori_loop(0, TILES // 8, build_tiles, 0)

    def spread_dual():
        top = jnp.max(dual[...], axis=1, keepdims=True)
        for n, part in enumerate(three(dual[...] - top + ROW_LIFT)):
            u_parts[n] = part
        wide = jnp.broadcast_to(top, (TILES, 128))
        for t in range(TILES):
            t_row[t] = wide[t : t + 1] - ROW_LIFT

        def fill(i, c):
            at = pl.ds(pl.multiple_of(i * 8, 8), 8)
            u1, u2, u3 = u_parts[0, at], u_parts[1, at], u_parts[2, at]
            for j in range(8):
                t = i * 8 + j
                first = jnp.where(
                    sub8w == 3, u1[j : j + 1], jnp.where(sub8w == 7, u2[j : j + 1], y_base[t, 0:8])
                )
                second = jnp.where(sub8w == 3, u3[j : j + 1], y_base[t, 8:16])
                y_table[t, 0:16] = jnp.concatenate([first, second], axis=0).astype(BF16)
            return c

        lax.fori_loop(0, TILES // 8, fill, 0)

    spread_dual()
    g_block[BLOCKS] = jnp.full((1, 128), NEGATIVE, F32)

    pl.semaphore_wait(barrier, DEVICES - 1)

    def local(src, dst, sem):
        pltpu.make_async_copy(src, dst, sem).start()

    def remote(src, dst, out_sem, in_sem, device):
        pltpu.make_async_remote_copy(
            src_ref=src, dst_ref=dst, send_sem=out_sem, recv_sem=in_sem,
            device_id=(device,), device_id_type=MESH,
        ).start()

    def arrived(ref, sem):
        pltpu.make_async_copy(ref, ref, sem).wait()

    def peers(g):
        return pl.ds(g * PEERS, PEERS)

    def slots(g):
        return pl.ds(g * WIDTH, WIDTH)

    def pair(q):
        return pl.ds(2 * q, 2)

    def exchange(g, sends):
        for j in range(PEERS):
            q = g * PEERS + j
            for out, into, out_sem, in_sem in sends(q):
                if j == 0:

                    @pl.when(g == 0)
                    def _():
                        local(out, into, in_sem)

                    @pl.when(g > 0)
                    def _():
                        remote(out, into, out_sem, in_sem, me ^ q)
                else:
                    remote(out, into, out_sem, in_sem, me ^ q)

    def send_positions(g, c):
        exchange(
            g,
            lambda q: (
                (ids.at[pair(q)], id_in.at[pair(q)], send.at[6], id_sem.at[g]),
                (pos_out.at[q], pos_in.at[q], send.at[0], pos_sem.at[g]),
            ),
        )
        return c

    lax.fori_loop(0, GROUPS, send_positions, 0)

    def build_x(q):
        a = three(jnp.where((sub8 == 3) | (sub8 == 7), 0.0, SCALE * (pos_in[q] - 0.5)))
        r = [pltpu.roll(v, 4, 0) for v in a]
        for n, (lo, hi) in enumerate(((a, r), (r, a))):
            quarters = (
                jnp.where(low, lo[0], hi[0]), jnp.where(low, lo[0], hi[1]),
                jnp.where(low, lo[1], hi[1]), jnp.where(low, lo[2], hi[2]),
            )
            base = jnp.concatenate(quarters, axis=0)
            x_base[2 * q + n] = base
            ones = (
                jnp.where((sub8 == 3) | (sub8 == 7), 1.0, quarters[0]),
                jnp.where(sub8 == 3, 1.0, quarters[1]),
            )
            x_row[2 * q + n] = jnp.concatenate(ones + quarters[2:], axis=0).astype(BF16)

    def return_pairs(g, out, into, out_sem, in_sem):
        exchange(g, lambda q: ((out.at[pair(q)], into.at[pair(q)], out_sem, in_sem.at[g]),))

    def tile_id(g, n):
        return names[g * WIDTH + n]

    def row_pass(step):
        def body(i, c):
            g = (i + 1) % GROUPS
            if step == 0:
                arrived(id_in.at[slots(g)], id_sem.at[g])
                for n in range(WIDTH):
                    names[g * WIDTH + n] = id_in[g * WIDTH + n][0, 0]
                arrived(pos_in.at[peers(g)], pos_sem.at[g])
                for j in range(PEERS):
                    build_x(g * PEERS + j)
            for n in range(WIDTH):
                s = g * WIDTH + n
                t = tile_id(g, n)
                e = outer(y_table[t], x_row[s])
                total = jnp.sum(jnp.exp2(e), axis=0, keepdims=True)
                row_out[step, s] = t_row[t] + jnp.log2(total)
            return_pairs(g, row_out.at[step], row_in.at[step], send.at[1 + step], row_sem.at[step])
            return c

        lax.fori_loop(0, GROUPS, body, 0)

    def particle_side(step):
        for g in range(GROUPS):
            arrived(row_in.at[step, slots(g)], row_sem.at[step, g])

        def of_blocks(i, c):
            for j in range(8):
                b = i * 8 + j
                row = [row_in[step, slot_at[K * b + k]] for k in range(K)]
                row = [jnp.where(k < live[b], v, NEGATIVE) for k, v in enumerate(row)]
                top = jnp.maximum(jnp.maximum(row[0], row[1]), jnp.maximum(row[2], row[3]))
                total = sum(jnp.exp2(v - top) for v in row)
                g_block[b] = jnp.log2(masses[b]) - (top + jnp.log2(total))
            return c

        lax.fori_loop(0, BLOCKS // 8, of_blocks, 0)

        def send_g(g, c):
            for n in range(WIDTH):
                s = g * WIDTH + n
                g_out[step, s] = g_block[block_of[s]]
            return_pairs(g, g_out.at[step], g_in.at[step], send.at[3 + step], g_sem.at[step])
            return c

        lax.fori_loop(0, GROUPS, send_g, 0)

    def column_pass(step):
        def body(g, best):
            arrived(g_in.at[step, slots(g)], g_sem.at[step, g])
            for part in range(WIDTH // 8):
                at = pl.ds(pl.multiple_of(g * WIDTH + part * 8, 8), 8)
                values = g_in[step, at].reshape(8, 128)
                top = jnp.max(values, axis=1, keepdims=True)
                g1, g2, g3 = three(values - top + COL_LIFT)
                g_top[at] = jnp.broadcast_to(top, (8, 128))
                sums = []
                for j in range(8):
                    n = part * 8 + j
                    s = g * WIDTH + n
                    t = tile_id(g, n)
                    second = jnp.where(sub8 == 7, g1[j : j + 1], x_base[s, 8:16])
                    third = jnp.where(
                        sub8 == 3, g2[j : j + 1], jnp.where(sub8 == 7, g3[j : j + 1], x_base[s, 16:24])
                    )
                    x = jnp.concatenate([x_base[s, 0:8], second, third, x_base[s, 24:32]], axis=0)
                    e = outer(x.astype(BF16), y_table[t])
                    sums.append(jnp.sum(jnp.exp2(e), axis=0, keepdims=True))
                    best = jnp.maximum(best, jnp.where(sub64 == t, values[j : j + 1], NEGATIVE))
                column[at] = jnp.concatenate(sums, axis=0)
            return best

        best = lax.fori_loop(0, GROUPS, body, jnp.full((TILES, 128), NEGATIVE, F32))
        level = jnp.max(best, axis=1, keepdims=True)
        wide = jnp.broadcast_to(level, (TILES, 128))
        for t in range(TILES):
            g_tile[t] = wide[t : t + 1]

        def scale(g, c):
            part, mask = [], []
            for half in range(2):
                at = pl.ds(pl.multiple_of(g * 16 + half * 8, 8), 8)
                named = [names[g * 16 + half * 8 + j] for j in range(8)]
                tops = jnp.concatenate([g_tile[t] for t in named], axis=0)
                factor = jnp.exp2(0.5 * (g_top[at] - tops))
                factor = jnp.concatenate([factor] * 4, axis=1)
                part.append(three(column[at] * factor * factor))
                name = jnp.full((8, 128), named[0], jnp.int32)
                for j in range(1, 8):
                    name = jnp.where(sub8 == j, named[j], name)
                mask.append(jnp.where(name == lane8, 1.0, 0.0))
            at = pl.ds(pl.multiple_of(g * 16, 16), 16)
            for n in range(3):
                parts[n, at] = jnp.concatenate([part[0][n], part[1][n]], axis=0).astype(BF16)
            owner_mask[at] = jnp.concatenate(mask, axis=0).astype(BF16)
            return c

        lax.fori_loop(0, SLOTS // 16, scale, 0)
        total = sum(outer(owner_mask[...], parts[n]) for n in range(3))[0:TILES]
        covered = level > 0.1 * NEGATIVE
        updated = log_sample[...] - (level - COL_LIFT + jnp.log2(jnp.where(covered, total, 1.0)))
        dual[...] = jnp.where(covered, updated, dual[...])
        spread_dual()

    for step in range(ITERS):
        row_pass(step)
        particle_side(step)
        column_pass(step)

    sub4 = lax.broadcasted_iota(jnp.int32, (4, 128), 0)

    def final(i, c):
        g = (i + 1) % GROUPS
        for n in range(WIDTH):
            s = g * WIDTH + n
            t = tile_id(g, n)
            y = y_table[t]
            weight = jnp.exp2(outer(y, x_row[s]))
            coarse = weight.astype(BF16)
            fine = (weight - coarse.astype(F32)).astype(BF16)
            sums = inner(y, coarse) + inner(y, fine)
            mass = sums[15:16]
            where = sums[0:4] + sums[4:8] + sums[8:12]
            fin_out[s] = jnp.where(sub4 == 3, t_row[t] + jnp.log2(mass), where / mass)
        return_pairs(g, fin_out, fin_in, send.at[5], fin_sem)
        return c

    lax.fori_loop(0, GROUPS, final, 0)
    for g in range(GROUPS):
        arrived(fin_in.at[slots(g)], fin_sem.at[g])

    def finish(i, c):
        for j in range(8):
            b = i * 8 + j
            got = [fin_in[slot_at[K * b + k]] for k in range(K)]
            row = [jnp.where(k < live[b], v[3:4], NEGATIVE) for k, v in enumerate(got)]
            top = jnp.maximum(jnp.maximum(row[0], row[1]), jnp.maximum(row[2], row[3]))
            weight = [jnp.exp2(v - top) for v in row]
            total = weight[0] + weight[1] + weight[2] + weight[3]
            centre[b] = sum(w * v for w, v in zip(weight, got)) / total
        return c

    lax.fori_loop(0, BLOCKS // 8, finish, 0)

    most = pl.ds(0, DEVICES - 1)
    rows = pl.ds(0, 2 * (DEVICES - 1))
    arrived(pos_out.at[most], send.at[0])
    arrived(ids.at[rows], send.at[6])
    for step in range(ITERS):
        arrived(row_out.at[step, rows], send.at[1 + step])
        arrived(g_out.at[step, rows], send.at[3 + step])
    arrived(fin_out.at[rows], send.at[5])


def local_step(
    positions, velocities, masses, samples, sample_mass, start_potential,
    route_owner, route_tile, live_count,
):
    me = lax.axis_index("dev")
    slots = BLOCKS * K
    owner = route_owner.reshape(slots)
    code = owner ^ me
    number = jnp.arange(slots, dtype=jnp.int32)
    alive = (jnp.arange(K, dtype=jnp.int32)[None, :] < live_count[:, None]).reshape(slots)
    same = (code[:, None] == code[None, :]) & alive[:, None] & (number[:, None] < number[None, :])
    place = 2 * code + jnp.sum(same.astype(jnp.int32), axis=0)
    slot_at = jnp.where(alive, place, 0)
    here = (jnp.arange(SLOTS, dtype=jnp.int32)[:, None] == place[None, :]) & alive[None, :]
    block_of = BLOCKS - jnp.sum(jnp.where(here, BLOCKS - number // K, 0), axis=1)
    named = jnp.sum(jnp.where(here, route_tile.reshape(slots)[None, :], 0), axis=1)
    ids = jnp.broadcast_to(named[:, None, None], (SLOTS, 1, 128))

    particles = positions.reshape(3, BLOCKS, BLK).transpose(1, 0, 2)
    tiles = samples.reshape(3, TILES, TILE).transpose(1, 0, 2)

    vmem, smem = pl.BlockSpec(memory_space=pltpu.VMEM), pl.BlockSpec(memory_space=pltpu.SMEM)
    dma = pltpu.SemaphoreType.DMA
    centre = pl.pallas_call(
        kernel,
        out_shape=jax.ShapeDtypeStruct((BLOCKS, 4, BLK), F32),
        in_specs=[smem] * 3 + [vmem] * 6,
        out_specs=vmem,
        scratch_shapes=[
            pltpu.VMEM((DEVICES, 8, 128), F32),
            pltpu.VMEM((DEVICES, 8, 128), F32),
            pltpu.VMEM((SLOTS, 1, 128), jnp.int32),
            pltpu.SMEM((SLOTS,), jnp.int32),
            pltpu.VMEM((ITERS, SLOTS, 1, 128), F32),
            pltpu.VMEM((ITERS, SLOTS, 1, 128), F32),
            pltpu.VMEM((ITERS, SLOTS, 1, 128), F32),
            pltpu.VMEM((ITERS, SLOTS, 1, 128), F32),
            pltpu.VMEM((SLOTS, 4, 128), F32),
            pltpu.VMEM((SLOTS, 4, 128), F32),
            pltpu.VMEM((SLOTS, 32, 128), BF16),
            pltpu.VMEM((SLOTS, 32, 128), F32),
            pltpu.VMEM((TILES, 32, TILE), BF16),
            pltpu.VMEM((TILES, 16, TILE), F32),
            pltpu.VMEM((TILES, TILE), F32),
            pltpu.VMEM((3, TILES, TILE), F32),
            pltpu.VMEM((TILES, 1, 128), F32),
            pltpu.VMEM((TILES, TILE), F32),
            pltpu.VMEM((BLOCKS + 1, 1, 128), F32),
            pltpu.VMEM((SLOTS, TILE), F32),
            pltpu.VMEM((SLOTS, 128), F32),
            pltpu.VMEM((TILES, 1, 128), F32),
            pltpu.VMEM((3, SLOTS, TILE), BF16),
            pltpu.VMEM((SLOTS, 128), BF16),
            dma((7,)),
            dma((GROUPS,)),
            dma((GROUPS,)),
            dma((ITERS, GROUPS)),
            dma((ITERS, GROUPS)),
            dma((GROUPS,)),
        ],
        compiler_params=pltpu.CompilerParams(
            collective_id=0, has_side_effects=True, vmem_limit_bytes=48 << 20
        ),
        cost_estimate=pl.CostEstimate(
            flops=5 * 64 * SLOTS * BLK * TILE,
            transcendentals=5 * SLOTS * BLK * TILE,
            bytes_accessed=2 << 20,
        ),
    )(
        block_of, slot_at, live_count, ids, particles, masses.reshape(BLOCKS, 1, BLK), tiles,
        start_potential.reshape(TILES, 1, TILE), sample_mass.reshape(TILES, 1, TILE),
    )

    middle = centre[:, 0:3].transpose(1, 0, 2).reshape(3, BLOCKS * BLK) + 0.5
    new_velocity = velocities + STIFFNESS * (middle - positions)
    return positions + TIMESTEP * new_velocity, new_velocity


def solution(mesh):
    across, along = P(None, "dev"), P("dev")
    return jax.shard_map(
        local_step,
        mesh=mesh,
        in_specs=(
            across, across, along, across, along, along, P("dev", None), P("dev", None), along
        ),
        out_specs=(across, across),
        check_vma=False,
    )
```

```python
import math

import jax
import jax.numpy as jnp
from jax import lax
from jax.experimental import pallas as pl
from jax.experimental.pallas import tpu as pltpu
from jax.sharding import PartitionSpec as P

MESH = pl.DeviceIdType.MESH
F32, BF16 = jnp.float32, jnp.bfloat16

BLK = 128
TILE = 512
K = 4
ITERS = 2
DEVICES = 128
BLOCKS = 32
TILES = 64
SLOTS = 2 * DEVICES
GROUPS = 4
PEERS = 32
WIDTH = 2 * PEERS

EPSILON = 0.01
STIFFNESS = 150.0
TIMESTEP = 0.05
SCALE = 1.0 / (EPSILON * math.log(2.0))
NEGATIVE = -1e30
ROW_LIFT = 8.0
COL_LIFT = 3.0


def outer(a, b):
    return lax.dot_general(a, b, (((0,), (0,)), ((), ())), preferred_element_type=F32)


def inner(a, b):
    return lax.dot_general(a, b, (((1,), (0,)), ((), ())), preferred_element_type=F32)


def three(v):
    first = v.astype(BF16).astype(F32)
    rest = v - first
    second = rest.astype(BF16).astype(F32)
    return first, second, (rest - second).astype(BF16).astype(F32)


def kernel(
    block_of, slot_at, live, ids, particles, masses, tiles, start, sample_mass,
    centre,
    pos_out, pos_in, id_in, names, row_out, row_in, g_out, g_in, fin_out, fin_in,
    x_row, x_base, y_table, y_base, dual, u_parts, t_row,
    log_sample, g_block, column, g_top, g_tile, parts, owner_mask,
    send, pos_sem, id_sem, row_sem, g_sem, fin_sem,
):
    me = lax.axis_index("dev")
    barrier = pltpu.get_barrier_semaphore()

    def greet(q, c):
        pl.semaphore_signal(barrier, inc=1, device_id=(me ^ q,), device_id_type=MESH)
        return c

    lax.fori_loop(1, DEVICES, greet, 0)

    sub8 = lax.broadcasted_iota(jnp.int32, (8, 128), 0)
    low = sub8 < 4
    sub8w = lax.broadcasted_iota(jnp.int32, (8, TILE), 0)
    loww = sub8w < 4
    lane8 = lax.broadcasted_iota(jnp.int32, (8, 128), 1)
    sub64 = lax.broadcasted_iota(jnp.int32, (TILES, 128), 0)

    blank = jnp.zeros((1, 128), F32)
    blankw = jnp.zeros((1, TILE), F32)

    def stage_positions(g, c):
        for j in range(PEERS):
            q = g * PEERS + j
            first, second = (
                particles[jnp.minimum(block_of[2 * q + n], BLOCKS - 1)] for n in range(2)
            )
            pos_out[q] = jnp.concatenate([first, blank, second, blank], axis=0)
        return c

    lax.fori_loop(0, GROUPS, stage_positions, 0)

    def build_tiles(i, c):
        duals, logs = [], []
        for j in range(8):
            t = i * 8 + j
            v = tiles[t] - 0.5
            duals.append(start[t] - 0.5 * jnp.sum(v * v, axis=0, keepdims=True))
            logs.append(sample_mass[t])
            b1, b2, b3 = three(jnp.concatenate([v, blankw, v, blankw], axis=0))
            y_base[t, 0:8] = jnp.where(loww, b1, b2)
            y_base[t, 8:16] = jnp.where(sub8w == 7, 1.0, jnp.where(loww, b3, b1))
            third = jnp.where((sub8w == 3) | (sub8w == 7), 1.0, jnp.where(loww, b2, b3))
            y_table[t, 16:32] = jnp.concatenate(
                [third, jnp.where(loww, b1, b2)], axis=0
            ).astype(BF16)
        at = pl.ds(pl.multiple_of(i * 8, 8), 8)
        dual[at] = SCALE * jnp.concatenate(duals, axis=0)
        log_sample[at] = jnp.log2(jnp.concatenate(logs, axis=0))
        return c

    lax.fori_loop(0, TILES // 8, build_tiles, 0)

    def spread_dual():
        top = jnp.max(dual[...], axis=1, keepdims=True)
        for n, part in enumerate(three(dual[...] - top + ROW_LIFT)):
            u_parts[n] = part
        wide = jnp.broadcast_to(top, (TILES, 128))
        for t in range(TILES):
            t_row[t] = wide[t : t + 1] - ROW_LIFT

        def fill(i, c):
            at = pl.ds(pl.multiple_of(i * 8, 8), 8)
            u1, u2, u3 = u_parts[0, at], u_parts[1, at], u_parts[2, at]
            for j in range(8):
                t = i * 8 + j
                first = jnp.where(
                    sub8w == 3, u1[j : j + 1], jnp.where(sub8w == 7, u2[j : j + 1], y_base[t, 0:8])
                )
                second = jnp.where(sub8w == 3, u3[j : j + 1], y_base[t, 8:16])
                y_table[t, 0:16] = jnp.concatenate([first, second], axis=0).astype(BF16)
            return c

        lax.fori_loop(0, TILES // 8, fill, 0)

    spread_dual()
    g_block[BLOCKS] = jnp.full((1, 128), NEGATIVE, F32)

    pl.semaphore_wait(barrier, DEVICES - 1)

    def local(src, dst, sem):
        pltpu.make_async_copy(src, dst, sem).start()

    def remote(src, dst, out_sem, in_sem, device):
        pltpu.make_async_remote_copy(
            src_ref=src, dst_ref=dst, send_sem=out_sem, recv_sem=in_sem,
            device_id=(device,), device_id_type=MESH,
        ).start()

    def arrived(ref, sem):
        pltpu.make_async_copy(ref, ref, sem).wait()

    def peers(g):
        return pl.ds(g * PEERS, PEERS)

    def slots(g):
        return pl.ds(g * WIDTH, WIDTH)

    def pair(q):
        return pl.ds(2 * q, 2)

    def exchange(g, sends):
        for j in range(PEERS):
            q = g * PEERS + j
            for out, into, out_sem, in_sem in sends(q):
                if j == 0:

                    @pl.when(g == 0)
                    def _():
                        local(out, into, in_sem)

                    @pl.when(g > 0)
                    def _():
                        remote(out, into, out_sem, in_sem, me ^ q)
                else:
                    remote(out, into, out_sem, in_sem, me ^ q)

    def send_positions(i, c):
        g = (i + 1) % GROUPS
        exchange(
            g,
            lambda q: (
                (ids.at[pair(q)], id_in.at[pair(q)], send.at[6], id_sem.at[g]),
                (pos_out.at[q], pos_in.at[q], send.at[0], pos_sem.at[g]),
            ),
        )
        return c

    lax.fori_loop(0, GROUPS, send_positions, 0)

    def build_x(q):
        a = three(jnp.where((sub8 == 3) | (sub8 == 7), 0.0, SCALE * (pos_in[q] - 0.5)))
        r = [pltpu.roll(v, 4, 0) for v in a]
        for n, (lo, hi) in enumerate(((a, r), (r, a))):
            quarters = (
                jnp.where(low, lo[0], hi[0]), jnp.where(low, lo[0], hi[1]),
                jnp.where(low, lo[1], hi[1]), jnp.where(low, lo[2], hi[2]),
            )
            base = jnp.concatenate(quarters, axis=0)
            x_base[2 * q + n] = base
            ones = (
                jnp.where((sub8 == 3) | (sub8 == 7), 1.0, quarters[0]),
                jnp.where(sub8 == 3, 1.0, quarters[1]),
            )
            x_row[2 * q + n] = jnp.concatenate(ones + quarters[2:], axis=0).astype(BF16)

    def return_pairs(g, out, into, out_sem, in_sem):
        exchange(g, lambda q: ((out.at[pair(q)], into.at[pair(q)], out_sem, in_sem.at[g]),))

    def tile_id(g, n):
        return names[g * WIDTH + n]

    def row_pass(step):
        def body(i, c):
            g = (i + 1) % GROUPS
            if step == 0:
                arrived(id_in.at[slots(g)], id_sem.at[g])
                for n in range(WIDTH):
                    names[g * WIDTH + n] = id_in[g * WIDTH + n][0, 0]
                arrived(pos_in.at[peers(g)], pos_sem.at[g])
                for j in range(PEERS):
                    build_x(g * PEERS + j)
            for n in range(WIDTH):
                s = g * WIDTH + n
                t = tile_id(g, n)
                e = outer(y_table[t], x_row[s])
                total = jnp.sum(jnp.exp2(e), axis=0, keepdims=True)
                row_out[step, s] = t_row[t] + jnp.log2(total)
            return_pairs(g, row_out.at[step], row_in.at[step], send.at[1 + step], row_sem.at[step])
            return c

        lax.fori_loop(0, GROUPS, body, 0)

    def particle_side(step):
        for g in range(GROUPS):
            arrived(row_in.at[step, slots(g)], row_sem.at[step, g])

        def of_blocks(i, c):
            for j in range(8):
                b = i * 8 + j
                row = [row_in[step, slot_at[K * b + k]] for k in range(K)]
                row = [jnp.where(k < live[b], v, NEGATIVE) for k, v in enumerate(row)]
                top = jnp.maximum(jnp.maximum(row[0], row[1]), jnp.maximum(row[2], row[3]))
                total = sum(jnp.exp2(v - top) for v in row)
                g_block[b] = jnp.log2(masses[b]) - (top + jnp.log2(total))
            return c

        lax.fori_loop(0, BLOCKS // 8, of_blocks, 0)

        def send_g(g, c):
            for n in range(WIDTH):
                s = g * WIDTH + n
                g_out[step, s] = g_block[block_of[s]]
            return_pairs(g, g_out.at[step], g_in.at[step], send.at[3 + step], g_sem.at[step])
            return c

        lax.fori_loop(0, GROUPS, send_g, 0)

    def column_pass(step):
        def body(g, best):
            arrived(g_in.at[step, slots(g)], g_sem.at[step, g])
            for part in range(WIDTH // 8):
                at = pl.ds(pl.multiple_of(g * WIDTH + part * 8, 8), 8)
                values = g_in[step, at].reshape(8, 128)
                top = jnp.max(values, axis=1, keepdims=True)
                g1, g2, g3 = three(values - top + COL_LIFT)
                g_top[at] = jnp.broadcast_to(top, (8, 128))
                sums = []
                for j in range(8):
                    n = part * 8 + j
                    s = g * WIDTH + n
                    t = tile_id(g, n)
                    second = jnp.where(sub8 == 7, g1[j : j + 1], x_base[s, 8:16])
                    third = jnp.where(
                        sub8 == 3, g2[j : j + 1], jnp.where(sub8 == 7, g3[j : j + 1], x_base[s, 16:24])
                    )
                    x = jnp.concatenate([x_base[s, 0:8], second, third, x_base[s, 24:32]], axis=0)
                    e = outer(x.astype(BF16), y_table[t])
                    sums.append(jnp.sum(jnp.exp2(e), axis=0, keepdims=True))
                    best = jnp.maximum(best, jnp.where(sub64 == t, values[j : j + 1], NEGATIVE))
                column[at] = jnp.concatenate(sums, axis=0)
            return best

        best = lax.fori_loop(0, GROUPS, body, jnp.full((TILES, 128), NEGATIVE, F32))
        level = jnp.max(best, axis=1, keepdims=True)
        wide = jnp.broadcast_to(level, (TILES, 128))
        for t in range(TILES):
            g_tile[t] = wide[t : t + 1]

        def scale(g, c):
            part, mask = [], []
            for half in range(2):
                at = pl.ds(pl.multiple_of(g * 16 + half * 8, 8), 8)
                named = [names[g * 16 + half * 8 + j] for j in range(8)]
                tops = jnp.concatenate([g_tile[t] for t in named], axis=0)
                factor = jnp.exp2(0.5 * (g_top[at] - tops))
                factor = jnp.concatenate([factor] * 4, axis=1)
                part.append(three(column[at] * factor * factor))
                name = jnp.full((8, 128), named[0], jnp.int32)
                for j in range(1, 8):
                    name = jnp.where(sub8 == j, named[j], name)
                mask.append(jnp.where(name == lane8, 1.0, 0.0))
            at = pl.ds(pl.multiple_of(g * 16, 16), 16)
            for n in range(3):
                parts[n, at] = jnp.concatenate([part[0][n], part[1][n]], axis=0).astype(BF16)
            owner_mask[at] = jnp.concatenate(mask, axis=0).astype(BF16)
            return c

        lax.fori_loop(0, SLOTS // 16, scale, 0)
        total = sum(outer(owner_mask[...], parts[n]) for n in range(3))[0:TILES]
        covered = level > 0.1 * NEGATIVE
        updated = log_sample[...] - (level - COL_LIFT + jnp.log2(jnp.where(covered, total, 1.0)))
        dual[...] = jnp.where(covered, updated, dual[...])
        spread_dual()

    for step in range(ITERS):
        row_pass(step)
        particle_side(step)
        column_pass(step)

    sub4 = lax.broadcasted_iota(jnp.int32, (4, 128), 0)

    def final(i, c):
        g = (i + 1) % GROUPS
        for n in range(WIDTH):
            s = g * WIDTH + n
            t = tile_id(g, n)
            y = y_table[t]
            weight = jnp.exp2(outer(y, x_row[s]))
            coarse = weight.astype(BF16)
            fine = (weight - coarse.astype(F32)).astype(BF16)
            sums = inner(y, coarse) + inner(y, fine)
            mass = sums[15:16]
            where = sums[0:4] + sums[4:8] + sums[8:12]
            fin_out[s] = jnp.where(sub4 == 3, t_row[t] + jnp.log2(mass), where / mass)
        return_pairs(g, fin_out, fin_in, send.at[5], fin_sem)
        return c

    lax.fori_loop(0, GROUPS, final, 0)
    for g in range(GROUPS):
        arrived(fin_in.at[slots(g)], fin_sem.at[g])

    def finish(i, c):
        for j in range(8):
            b = i * 8 + j
            got = [fin_in[slot_at[K * b + k]] for k in range(K)]
            row = [jnp.where(k < live[b], v[3:4], NEGATIVE) for k, v in enumerate(got)]
            top = jnp.maximum(jnp.maximum(row[0], row[1]), jnp.maximum(row[2], row[3]))
            weight = [jnp.exp2(v - top) for v in row]
            total = weight[0] + weight[1] + weight[2] + weight[3]
            centre[b] = sum(w * v for w, v in zip(weight, got)) / total
        return c

    lax.fori_loop(0, BLOCKS // 8, finish, 0)

    most = pl.ds(0, DEVICES - 1)
    rows = pl.ds(0, 2 * (DEVICES - 1))
    arrived(pos_out.at[most], send.at[0])
    arrived(ids.at[rows], send.at[6])
    for step in range(ITERS):
        arrived(row_out.at[step, rows], send.at[1 + step])
        arrived(g_out.at[step, rows], send.at[3 + step])
    arrived(fin_out.at[rows], send.at[5])


def local_step(
    positions, velocities, masses, samples, sample_mass, start_potential,
    route_owner, route_tile, live_count,
):
    me = lax.axis_index("dev")
    slots = BLOCKS * K
    owner = route_owner.reshape(slots)
    code = owner ^ me
    number = jnp.arange(slots, dtype=jnp.int32)
    alive = (jnp.arange(K, dtype=jnp.int32)[None, :] < live_count[:, None]).reshape(slots)
    same = (code[:, None] == code[None, :]) & alive[:, None] & (number[:, None] < number[None, :])
    place = 2 * code + jnp.sum(same.astype(jnp.int32), axis=0)
    slot_at = jnp.where(alive, place, 0)
    here = (jnp.arange(SLOTS, dtype=jnp.int32)[:, None] == place[None, :]) & alive[None, :]
    block_of = BLOCKS - jnp.sum(jnp.where(here, BLOCKS - number // K, 0), axis=1)
    named = jnp.sum(jnp.where(here, route_tile.reshape(slots)[None, :], 0), axis=1)
    ids = jnp.broadcast_to(named[:, None, None], (SLOTS, 1, 128))

    particles = positions.reshape(3, BLOCKS, BLK).transpose(1, 0, 2)
    tiles = samples.reshape(3, TILES, TILE).transpose(1, 0, 2)

    vmem, smem = pl.BlockSpec(memory_space=pltpu.VMEM), pl.BlockSpec(memory_space=pltpu.SMEM)
    dma = pltpu.SemaphoreType.DMA
    centre = pl.pallas_call(
        kernel,
        out_shape=jax.ShapeDtypeStruct((BLOCKS, 4, BLK), F32),
        in_specs=[smem] * 3 + [vmem] * 6,
        out_specs=vmem,
        scratch_shapes=[
            pltpu.VMEM((DEVICES, 8, 128), F32),
            pltpu.VMEM((DEVICES, 8, 128), F32),
            pltpu.VMEM((SLOTS, 1, 128), jnp.int32),
            pltpu.SMEM((SLOTS,), jnp.int32),
            pltpu.VMEM((ITERS, SLOTS, 1, 128), F32),
            pltpu.VMEM((ITERS, SLOTS, 1, 128), F32),
            pltpu.VMEM((ITERS, SLOTS, 1, 128), F32),
            pltpu.VMEM((ITERS, SLOTS, 1, 128), F32),
            pltpu.VMEM((SLOTS, 4, 128), F32),
            pltpu.VMEM((SLOTS, 4, 128), F32),
            pltpu.VMEM((SLOTS, 32, 128), BF16),
            pltpu.VMEM((SLOTS, 32, 128), F32),
            pltpu.VMEM((TILES, 32, TILE), BF16),
            pltpu.VMEM((TILES, 16, TILE), F32),
            pltpu.VMEM((TILES, TILE), F32),
            pltpu.VMEM((3, TILES, TILE), F32),
            pltpu.VMEM((TILES, 1, 128), F32),
            pltpu.VMEM((TILES, TILE), F32),
            pltpu.VMEM((BLOCKS + 1, 1, 128), F32),
            pltpu.VMEM((SLOTS, TILE), F32),
            pltpu.VMEM((SLOTS, 128), F32),
            pltpu.VMEM((TILES, 1, 128), F32),
            pltpu.VMEM((3, SLOTS, TILE), BF16),
            pltpu.VMEM((SLOTS, 128), BF16),
            dma((7,)),
            dma((GROUPS,)),
            dma((GROUPS,)),
            dma((ITERS, GROUPS)),
            dma((ITERS, GROUPS)),
            dma((GROUPS,)),
        ],
        compiler_params=pltpu.CompilerParams(
            collective_id=0, has_side_effects=True, vmem_limit_bytes=48 << 20
        ),
        cost_estimate=pl.CostEstimate(
            flops=5 * 64 * SLOTS * BLK * TILE,
            transcendentals=5 * SLOTS * BLK * TILE,
            bytes_accessed=2 << 20,
        ),
    )(
        block_of, slot_at, live_count, ids, particles, masses.reshape(BLOCKS, 1, BLK), tiles,
        start_potential.reshape(TILES, 1, TILE), sample_mass.reshape(TILES, 1, TILE),
    )

    middle = centre[:, 0:3].transpose(1, 0, 2).reshape(3, BLOCKS * BLK) + 0.5
    new_velocity = velocities + STIFFNESS * (middle - positions)
    return positions + TIMESTEP * new_velocity, new_velocity


def solution(mesh):
    across, along = P(None, "dev"), P("dev")
    return jax.shard_map(
        local_step,
        mesh=mesh,
        in_specs=(
            across, across, along, across, along, along, P("dev", None), P("dev", None), along
        ),
        out_specs=(across, across),
        check_vma=False,
    )
```
